32 devices in a mesh: groups: 2 (over y), mesh: 8 (over z, x), noise: 2 (over core).
Axes of the slice: x: 2, y: 2, z: 4, core: 2. Of those that a mesh axis runs over, the one named last changes fastest.
Arguments:
- inputs: bfloat16 [4, 4096, 512], P(('groups', 'noise'), 'mesh'), parts along dimension 0, may hold values from -6 to 6
- norm_gain: float32 [512], replicated, may hold values from 0.1 to 1.9
- qkv_weight: bfloat16 [512, 1536], replicated, may hold values from -3 to 3
- neighbours: int32 [32, 6], replicated, may hold values from 0 to 31, as said below
- out_grad: bfloat16 [4, 4096, 512], P(('groups', 'noise'), 'mesh'), parts along dimension 0, may hold values from -6 to 6
Outputs:
- input_grad: bfloat16 [4, 4096, 512], P(('groups', 'noise'), 'mesh'), parts along dimension 0
- weight_grad: float32 [1024, 1536], P(('groups', 'mesh')), parts along dimension 0
- gain_grad: float32 [1024], P(('groups', 'mesh')), parts along dimension 0
The draws below stay inside these ranges and needn't reach their ends.
There are 2 independent parts, one for each index of `groups`. The reference program is written for one: setup_inputs(seed, part) draws one part's arguments, and reference() takes and returns one part's arrays. A program takes and returns all parts, laid end to end along the dimension named above; an argument that names none is the same for every part. Nothing has to cross between parts.
Inputs may be any that keep to these rules, and one draw needn't show every extreme that they name: `neighbours`: row b lists block b first, then 6 - 1 other distinct blocks. Block c belongs to device c // 4 of mesh; every listed block belongs to a device at most 2 places away from the device of b. The blocks of one device list at most 2 distinct blocks of any one other device, and exactly 2 for some pair of devices.
All inputs are finite; a program needn't handle non-finite values.
Results may differ from the reference program's by a relative error of at most 0.0091.
Values may be sent and summed in bfloat16 or wider, within the bound.
A program may use at most 64 MiB of HBM per device.

```python
import math
import jax
import jax.numpy as jnp
from jax import lax

D = 512
HEADS = 4
BS = 128
KHOP = 6
REACH = 2
CAP = 2
BLK_DEV = 4
NBLK = 32
NODES = 4096
SAMPLES = 2
N_MESH = 8


def draw_qkv_weight(key, part):
    key = jax.random.fold_in(key, 5)
    main_key = jax.random.fold_in(key, 0)
    whole = jax.random.normal(main_key, (D, 3 * D), jnp.float32) / math.sqrt(D)
    return jnp.clip(whole, -3.0, 3.0).astype(jnp.bfloat16)


def draw_neighbours(key, part):
    key = jax.random.fold_in(key, 11)
    count_key, order_key = jax.random.split(key, 2)
    offsets = jnp.array([shift_by for shift_by in range(-REACH, REACH + 1) if shift_by != 0], jnp.int32)
    devices = jnp.arange(N_MESH, dtype=jnp.int32)
    holders = devices[:, None] + offsets[None, :]
    valid = (holders >= 0) & (holders < N_MESH)
    counts = jax.random.randint(count_key, (N_MESH, 2 * REACH), 1, CAP + 1)
    counts = counts.at[0, REACH].set(CAP)
    counts = jnp.where(valid, counts, 0)
    order_keys = jax.random.split(order_key, N_MESH * 2 * REACH)
    orders = jax.vmap(lambda single: jax.random.permutation(single, BLK_DEV))(order_keys)
    orders = orders.reshape(N_MESH, 2 * REACH, BLK_DEV).astype(jnp.int32)
    picked = holders[:, :, None] * BLK_DEV + orders[:, :, :CAP]
    live = valid[:, :, None] & (jnp.arange(CAP, dtype=jnp.int32)[None, None, :] < counts[:, :, None])
    picked = picked.reshape(N_MESH, 2 * REACH * CAP)
    live = live.reshape(N_MESH, 2 * REACH * CAP)
    packing = jnp.argsort(1 - live.astype(jnp.int32), axis=1, stable=True)
    remote = jnp.take_along_axis(picked, packing, axis=1)
    pool = jnp.sum(live.astype(jnp.int32), axis=1)
    per_row = jnp.minimum(pool, KHOP - 2)
    block_range = jnp.arange(BLK_DEV, dtype=jnp.int32)
    column = jnp.arange(KHOP - 1, dtype=jnp.int32)
    spot = (block_range[None, :, None] * per_row[:, None, None] + column[None, None, :]) % pool[:, None, None]
    far = jax.vmap(lambda listing, place: listing[place])(remote, spot)
    near = devices[:, None, None] * BLK_DEV + (block_range[None, :, None] + 1 + column[None, None, :] - per_row[:, None, None]) % BLK_DEV
    others = jnp.where(column[None, None, :] < per_row[:, None, None], far, near)
    selfs = devices[:, None] * BLK_DEV + block_range[None, :]
    rows = jnp.concatenate([selfs[:, :, None], others], axis=2).reshape(N_MESH * BLK_DEV, KHOP)
    return rows.astype(jnp.int32)


def block_scale(rng, shape, cuts, smallest, top_value):
    def one(dim, blocks):
        steps = jax.random.uniform(jax.random.fold_in(jax.random.fold_in(rng, 6), dim), (blocks,), jnp.float32, smallest / len(cuts), top_value / len(cuts))
        return jnp.repeat(jnp.exp(steps), shape[dim] // blocks).reshape((-1,) + (1,) * (len(shape) - dim - 1))

    gain = one(*cuts[0])
    for cut in cuts[1:]:
        gain = gain * one(*cut)
    return gain


def normal_values(own_key, shape, spread, bound, cuts=(), kind=jnp.bfloat16):
    level = block_scale(own_key, shape, cuts, -0.22, 0.18) if cuts else 1.0
    entries = jax.random.normal(own_key, shape, jnp.float32) * spread * level
    return jnp.minimum(jnp.maximum(entries, -bound), bound).astype(kind)


def setup_inputs(seed: int = 0, part: int = 0) -> dict:
    arg_keys = jax.random.split(jax.random.key(seed), 6)
    own_keys = jax.random.split(jax.random.fold_in(arg_keys[5], part), 6)
    return {
        "inputs": normal_values(own_keys[0], (SAMPLES, NODES, D), 1.0, 6.0, ((0, 2), (1, 8))),
        "norm_gain": jnp.clip(1.0 + 0.18 * jax.random.normal(arg_keys[1], (D,), jnp.float32), 0.1, 1.9),
        "qkv_weight": draw_qkv_weight(jax.random.fold_in(arg_keys[5], 71), part),
        "neighbours": draw_neighbours(jax.random.fold_in(arg_keys[5], 71), part),
        "out_grad": normal_values(own_keys[4], (SAMPLES, NODES, D), 1.0, 6.0, ((0, 2), (1, 8))),
    }


EPSILON = 1e-05

def reference(inputs, norm_gain, qkv_weight, neighbours, out_grad):
    samples = inputs.shape[0]
    head_dim = D // HEADS
    score_scale = 1.0 / math.sqrt(head_dim)
    as_float = inputs.astype(jnp.float32)
    centred = as_float - lax.optimization_barrier(jnp.mean(as_float, axis=-1, keepdims=True))
    inv_std = lax.rsqrt(lax.optimization_barrier(jnp.mean(centred * centred, axis=-1, keepdims=True)) + EPSILON)
    unit_rows = centred * inv_std
    normed = (unit_rows * norm_gain).astype(jnp.bfloat16)
    normed_rows = normed.reshape(samples * NODES, D)
    projected = jnp.dot(normed_rows, qkv_weight, preferred_element_type=jnp.float32).astype(jnp.bfloat16)
    projected = projected.reshape(samples, NBLK, BS, 3, HEADS, head_dim)
    queries = projected[:, :, :, 0]
    pairs = projected[:, :, :, 1:]
    grads = out_grad.reshape(samples, NBLK, BS, HEADS, head_dim)
    highest = lax.Precision.HIGHEST

    def device_step(grand_total, holder):
        first_block = (holder * BLK_DEV).astype(jnp.int32)
        rows = lax.dynamic_slice_in_dim(neighbours, first_block, BLK_DEV, 0)
        query_blk = lax.dynamic_slice_in_dim(queries, first_block, BLK_DEV, 1).astype(jnp.float32)
        grad_blk = lax.dynamic_slice_in_dim(grads, first_block, BLK_DEV, 1).astype(jnp.float32)
        slot_ids = rows.reshape(-1).astype(jnp.int32)
        listed = pairs[:, slot_ids].reshape(samples, BLK_DEV, KHOP, BS, 2, HEADS, head_dim).astype(jnp.float32)
        key_part = listed[:, :, :, :, 0]
        value_part = listed[:, :, :, :, 1]
        scores = jnp.einsum('sbqhd,sbjkhd->sbhqjk', query_blk, key_part, precision=highest) * score_scale
        flat_scores = scores.reshape(samples, BLK_DEV, HEADS, BS, KHOP * BS)
        row_max = lax.optimization_barrier(jnp.max(flat_scores, axis=-1, keepdims=True))
        powers = jnp.exp(flat_scores - row_max)
        attend = (powers / lax.optimization_barrier(jnp.sum(powers, axis=-1, keepdims=True))).reshape(scores.shape)
        attend_low = lax.optimization_barrier(attend.astype(jnp.bfloat16)).astype(jnp.float32)
        attended = jnp.einsum('sbhqjk,sbjkhd->sbqhd', attend_low, value_part, precision=highest)
        row_dot = lax.optimization_barrier(jnp.sum(grad_blk * attended, axis=-1)).transpose(0, 1, 3, 2)
        grad_attend = jnp.einsum('sbqhd,sbjkhd->sbhqjk', grad_blk, value_part, precision=highest)
        grad_scores = attend * (grad_attend - row_dot[..., None, None])
        grad_low = lax.optimization_barrier(grad_scores.astype(jnp.bfloat16)).astype(jnp.float32)
        query_grad = jnp.einsum('sbhqjk,sbjkhd->sbqhd', grad_low, key_part, precision=highest) * score_scale
        key_grad = jnp.einsum('sbhqjk,sbqhd->sbjkhd', grad_low, query_blk, precision=highest) * score_scale
        value_grad = jnp.einsum('sbhqjk,sbqhd->sbjkhd', attend_low, grad_blk, precision=highest)
        terms = jnp.stack([key_grad, value_grad], axis=4).reshape(samples, BLK_DEV * KHOP, BS, 2, HEADS, head_dim)
        same_id = slot_ids[:, None] == slot_ids[None, :]
        partial_value = jnp.einsum('im,smkchd->sikchd', same_id.astype(jnp.float32), terms, precision=highest)
        partial_value = lax.optimization_barrier(partial_value.astype(jnp.bfloat16)).astype(jnp.float32)
        first_seen = jnp.logical_not(jnp.any(jnp.tril(same_id, -1), axis=1))
        partial_value = jnp.where(first_seen[None, :, None, None, None, None], partial_value, jnp.float32(0.0))
        grand_total = grand_total.at[:, slot_ids].add(partial_value)
        return (grand_total, query_grad)
    start_total = jnp.zeros((samples, NBLK, BS, 2, HEADS, head_dim), jnp.float32)
    pair_total, query_grads = lax.scan(device_step, start_total, jnp.arange(N_MESH, dtype=jnp.int32))
    query_grads = query_grads.transpose(1, 0, 2, 3, 4, 5).reshape(samples, NBLK, BS, HEADS, head_dim)
    grad_rows = jnp.concatenate([query_grads[:, :, :, None], pair_total], axis=3)
    grad_rows = grad_rows.astype(jnp.bfloat16).reshape(samples * NODES, 3 * D)
    grad_scale = 1.0 / math.sqrt(samples * NODES)
    weight_grad = jnp.dot(normed_rows.T, grad_rows, preferred_element_type=jnp.float32) * grad_scale
    normed_grad = jnp.dot(grad_rows, qkv_weight.T, preferred_element_type=jnp.float32).reshape(samples, NODES, D)
    gain_grad = lax.optimization_barrier(jnp.sum(normed_grad * unit_rows, axis=(0, 1))) * grad_scale
    unit_grad = normed_grad * norm_gain
    input_grad = inv_std * (unit_grad - lax.optimization_barrier(jnp.mean(unit_grad, axis=-1, keepdims=True)) - unit_rows * lax.optimization_barrier(jnp.mean(unit_grad * unit_rows, axis=-1, keepdims=True)))
    return (input_grad.astype(jnp.bfloat16), weight_grad, gain_grad)
```

```python
import functools
import math

import jax
import jax.numpy as jnp
from jax import lax
from jax.experimental import pallas as pl
from jax.experimental.pallas import tpu as pltpu
from jax.sharding import PartitionSpec as P

HEADS = 4
BS = 128
KHOP = 6
BLK = 4
CAP = 2
EPSILON = 1e-05
OFFSETS = (-2, -1, 1, 2)
TABLE = BLK + CAP * len(OFFSETS)
MESH = pl.DeviceIdType.MESH
F32 = jnp.float32
BF16 = jnp.bfloat16


def dot(a, b, dims):
    return lax.dot_general(a, b, (dims, ((), ())), preferred_element_type=F32)


def layer_norm(rows):
    as_float = rows.astype(F32)
    centred = as_float - jnp.mean(as_float, axis=-1, keepdims=True)
    inv_std = lax.rsqrt(jnp.mean(centred * centred, axis=-1, keepdims=True) + EPSILON)
    return centred * inv_std, inv_std


def pick_two(hits):
    first = jnp.int32(BLK - 1)
    for c in reversed(range(BLK - 1)):
        first = jnp.where(hits[c], c, first)
    second = jnp.int32(0)
    for c in reversed(range(1, BLK)):
        second = jnp.where(jnp.logical_and(hits[c], first < c), c, second)
    return first, second


def listed_flags(rows, device):
    flags = []
    for c in range(BLK):
        flag = rows[0] == device * BLK + c
        for entry in rows[1:]:
            flag = jnp.logical_or(flag, entry == device * BLK + c)
        flags.append(flag)
    return flags


def kernel(
    n, grad_scale, fused_sum,
    neigh, x, gain, w, og,
    *refs,
):
    outs, scratch = refs[:3], refs[3:]
    dx, w_out, gain_out = outs
    (send, halo, unit, inv, normed_t, q, kv, dq, dkv, terms, own_ng, ret_send, ret,
     halo_ss, halo_rs, ret_ss, ret_rs) = scratch[:17]
    me = lax.axis_index("mesh")
    core = lax.axis_index("noise")
    d = x.shape[-1]
    hd = d // HEADS
    rows_dev = BLK * BS
    scale = 1.0 / math.sqrt(hd)
    rows_out = d // n

    def exists(oi):
        other = me + OFFSETS[oi]
        return jnp.logical_and(other >= 0, other < n)

    barrier = pltpu.get_barrier_semaphore()
    if fused_sum:
        for k in range(1, n):
            pl.semaphore_signal(barrier, inc=1, device_id={"mesh": lax.rem(me + k, n)}, device_id_type=MESH)
        pl.semaphore_signal(barrier, inc=1, device_id={"noise": 1 - core}, device_id_type=MESH)
    else:
        for oi in range(len(OFFSETS)):
            @pl.when(exists(oi))
            def _():
                pl.semaphore_signal(barrier, inc=1, device_id={"mesh": me + OFFSETS[oi]}, device_id_type=MESH)

    wanted = []
    for oi, off in enumerate(OFFSETS):
        other = jnp.clip(me + off, 0, n - 1)
        entries = [neigh[other * BLK + b, j] for b in range(BLK) for j in range(KHOP)]
        flags = listed_flags(entries, me)
        first, second = pick_two(flags)
        wanted.append((flags, first, second))
        send[oi, 0] = x[first]
        send[oi, 1] = x[second]

    if fused_sum:
        pl.semaphore_wait(barrier, n)
    else:
        for oi in range(len(OFFSETS)):
            @pl.when(exists(oi))
            def _():
                pl.semaphore_wait(barrier, 1)

    def halo_copy(oi):
        return pltpu.make_async_remote_copy(
            src_ref=send.at[oi], dst_ref=halo.at[3 - oi],
            send_sem=halo_ss.at[oi], recv_sem=halo_rs.at[3 - oi],
            device_id={"mesh": me + OFFSETS[oi]}, device_id_type=MESH)

    def halo_arrival(oi):
        return pltpu.make_async_remote_copy(
            src_ref=send.at[oi], dst_ref=halo.at[oi],
            send_sem=halo_ss.at[oi], recv_sem=halo_rs.at[oi],
            device_id={"mesh": me + OFFSETS[oi]}, device_id_type=MESH)

    for oi in (0, 3, 1, 2):
        @pl.when(exists(oi))
        def _():
            halo_copy(oi).start()

        @pl.when(jnp.logical_not(exists(oi)))
        def _():
            halo[oi] = jnp.zeros(halo.shape[1:], BF16)

    mine = [[neigh[me * BLK + b, j] for j in range(KHOP)] for b in range(BLK)]
    flat = [entry for row in mine for entry in row]
    table_id = [me * BLK + c for c in range(BLK)]
    for oi, off in enumerate(OFFSETS):
        flags = listed_flags(flat, me + off)
        first, second = pick_two(flags)
        base = (me + off) * BLK
        table_id.append(jnp.where(functools.reduce(jnp.logical_or, flags), base + first, -1))
        table_id.append(jnp.where(second > 0, base + second, -1))
    where_from = [[None] * KHOP for _ in range(BLK)]
    back = [[None] * BLK for _ in range(TABLE)]
    none = BLK * KHOP
    for b in range(BLK):
        spots = [jnp.int32(0)] * KHOP
        for t in range(TABLE):
            found = jnp.int32(none)
            for j in range(KHOP):
                same = mine[b][j] == table_id[t]
                spots[j] = jnp.where(same, t, spots[j])
                found = jnp.where(same, b * KHOP + j, found)
            back[t][b] = found
        where_from[b] = spots

    gain_row = gain[...]

    for t in range(BLK):
        u, istd = layer_norm(x[t])
        unit[t * BS:(t + 1) * BS, :] = u
        inv[t * BS:(t + 1) * BS, :] = istd
        normed = (u * gain_row).astype(BF16)
        normed_t[:, t * BS:(t + 1) * BS] = normed.T
        q[t] = dot(normed, w[:, :d], ((1,), (0,))).astype(BF16)
        kv[t] = dot(normed, w[:, d:], ((1,), (0,))).astype(BF16)
    for s in range(2):
        terms[s, none] = jnp.zeros(terms.shape[2:], F32)
    ret[CAP * len(OFFSETS)] = jnp.zeros(ret.shape[1:], BF16)

    for oi in (1, 2, 0, 3):
        @pl.when(exists(oi))
        def _():
            halo_arrival(oi).wait_recv()
        for slot in range(CAP):
            t = BLK + CAP * oi + slot
            u, _istd = layer_norm(halo[oi, slot])
            unit[t * BS:(t + 1) * BS, :] = u
            normed = (u * gain_row).astype(BF16)
            normed_t[:, t * BS:(t + 1) * BS] = normed.T
            kv[t] = dot(normed, w[:, d:], ((1,), (0,))).astype(BF16)

    if fused_sum:
        (chunk, sib, parts, gchunk, gsib, gparts, done, gdone,
         sib_ss, sib_rs, part_ss, part_rs, done_ss, done_rs) = scratch[17:]

        def bufs(c):
            if c < HEADS:
                return chunk.at[c], sib.at[c], parts.at[c], done.at[c]
            return gchunk, gsib, gparts, gdone

        def to_sibling(c):
            mine_c, sib_c, _parts, _done = bufs(c)
            return pltpu.make_async_remote_copy(
                src_ref=mine_c, dst_ref=sib_c, send_sem=sib_ss.at[c], recv_sem=sib_rs.at[c],
                device_id={"noise": 1 - core}, device_id_type=MESH)

        def to_peer(c, k):
            mine_c, _sib, parts_c, _done = bufs(c)
            peer = lax.rem(me + k, n)
            return pltpu.make_async_remote_copy(
                src_ref=mine_c.at[pl.ds(pl.multiple_of(peer * rows_out, rows_out), rows_out), :],
                dst_ref=parts_c.at[k], send_sem=part_ss.at[c, k], recv_sem=part_rs.at[c, k],
                device_id={"mesh": peer}, device_id_type=MESH)

        def final_copy(c):
            _mine, _sib, _parts, done_c = bufs(c)
            return pltpu.make_async_remote_copy(
                src_ref=done_c, dst_ref=done_c, send_sem=done_ss.at[c], recv_sem=done_rs.at[c],
                device_id={"noise": 1 - core}, device_id_type=MESH)

        def begin(c):
            @pl.when(core != c % 2)
            def _():
                to_sibling(c).start()

        def spread(c):
            @pl.when(core == c % 2)
            def _():
                mine_c, sib_c, parts_c, _done = bufs(c)
                to_sibling(c).wait_recv()
                total = mine_c[...].astype(F32) + sib_c[...].astype(F32)
                mine_c[...] = total.astype(BF16)
                for k in range(1, n):
                    to_peer(c, k).start()

        def gather(c):
            @pl.when(core == c % 2)
            def _():
                mine_c, _sib, parts_c, done_c = bufs(c)
                total = mine_c[pl.ds(pl.multiple_of(me * rows_out, rows_out), rows_out), :].astype(F32)
                for k in range(1, n):
                    to_peer(c, k).wait_recv()
                    total = total + parts_c[k].astype(F32)
                done_c[...] = total
                final_copy(c).start()

        def finish(c):
            @pl.when(core == c % 2)
            def _():
                final_copy(c).wait_send()
                for k in range(1, n):
                    to_peer(c, k).wait_send()

            @pl.when(core != c % 2)
            def _():
                to_sibling(c).wait_send()
                final_copy(c).wait_recv()
            _mine, _sib, _parts, done_c = bufs(c)
            if c < HEADS:
                for part in range(3):
                    w_out[:, part * d + c * hd:part * d + (c + 1) * hd] = done_c[:, part * hd:(part + 1) * hd]
            else:
                gain_out[...] = done_c[...]

    for h in range(HEADS):
        lo, hi = h * hd, (h + 1) * hd
        buf = h % 2
        for b in range(BLK):
            kg = jnp.concatenate([kv[where_from[b][j], :, lo:hi] for j in range(KHOP)], axis=0)
            vg = jnp.concatenate([kv[where_from[b][j], :, d + lo:d + hi] for j in range(KHOP)], axis=0)
            qh = q[b, :, lo:hi]
            gh = og[b, :, lo:hi]
            s = dot(kg, qh, ((1,), (1,)))
            top = jnp.max(s, axis=0, keepdims=True)
            p = jnp.exp2((s - top) * (scale * math.log2(math.e)))
            a = p * (1.0 / jnp.sum(p, axis=0, keepdims=True))
            a_low = a.astype(BF16)
            da = dot(vg, gh, ((1,), (1,)))
            row_dot = jnp.sum(a_low.astype(F32) * da, axis=0, keepdims=True)
            ds = (a * (da - row_dot)).astype(BF16)
            dq[b * BS:(b + 1) * BS, lo:hi] = (dot(ds, kg, ((0,), (0,))) * scale).astype(BF16)
            dk = dot(ds, qh, ((1,), (0,))) * scale
            dv = dot(a_low, gh, ((1,), (0,)))
            for j in range(KHOP):
                terms[buf, b * KHOP + j, :, :hd] = dk[j * BS:(j + 1) * BS]
                terms[buf, b * KHOP + j, :, hd:] = dv[j * BS:(j + 1) * BS]
        for t in range(TABLE):
            total = terms[buf, back[t][0]]
            for b in range(1, BLK):
                total = total + terms[buf, back[t][b]]
            dkv[t * BS:(t + 1) * BS, lo:hi] = total[:, :hd].astype(BF16)
            dkv[t * BS:(t + 1) * BS, d + lo:d + hi] = total[:, hd:].astype(BF16)
        wq = dot(normed_t[:, :rows_dev], dq[:, lo:hi], ((1,), (0,))) * grad_scale
        kv_cols = jnp.concatenate([dkv[:, lo:hi], dkv[:, d + lo:d + hi]], axis=1)
        wkv = dot(normed_t[...], kv_cols, ((1,), (0,))) * grad_scale
        if fused_sum:
            chunk[h, :, :hd] = wq.astype(BF16)
            chunk[h, :, hd:] = wkv.astype(BF16)
            begin(h)
            if h >= 1:
                spread(h - 1)
        else:
            w_out[:, lo:hi] = wq
            w_out[:, d + lo:d + hi] = wkv[:, :hd]
            w_out[:, 2 * d + lo:2 * d + hi] = wkv[:, hd:]

    def ret_copy(oi):
        return pltpu.make_async_remote_copy(
            src_ref=ret_send.at[oi], dst_ref=ret.at[pl.ds(CAP * (3 - oi), CAP)],
            send_sem=ret_ss.at[oi], recv_sem=ret_rs.at[3 - oi],
            device_id={"mesh": me + OFFSETS[oi]}, device_id_type=MESH)

    def ret_arrival(oi):
        return pltpu.make_async_remote_copy(
            src_ref=ret_send.at[oi], dst_ref=ret.at[pl.ds(CAP * oi, CAP)],
            send_sem=ret_ss.at[oi], recv_sem=ret_rs.at[oi],
            device_id={"mesh": me + OFFSETS[oi]}, device_id_type=MESH)

    gain_sum = jnp.zeros((1, d), F32)
    for oi in (0, 3, 1, 2):
        r0 = (BLK + CAP * oi) * BS
        ng = dot(dkv[r0:r0 + CAP * BS, :], w[:, d:], ((1,), (1,)))
        gain_sum += jnp.sum(ng * unit[r0:r0 + CAP * BS, :], axis=0, keepdims=True)
        for slot in range(CAP):
            ret_send[oi, slot] = ng[slot * BS:(slot + 1) * BS].astype(BF16)

        @pl.when(exists(oi))
        def _():
            ret_copy(oi).start()
    if fused_sum:
        spread(HEADS - 1)
    ng = dot(dq[...], w[:, :d], ((1,), (1,))) + dot(dkv[:rows_dev, :], w[:, d:], ((1,), (1,)))
    own_ng[...] = ng
    gain_sum += jnp.sum(ng * unit[:rows_dev, :], axis=0, keepdims=True)
    gain_sum = gain_sum * grad_scale
    if fused_sum:
        gchunk[...] = jnp.broadcast_to(gain_sum, (BS, d)).T.astype(BF16)
        begin(HEADS)
        for c in range(HEADS - 1):
            gather(c)
        spread(HEADS)
    else:
        gain_out[...] = gain_sum

    for oi in range(len(OFFSETS)):
        @pl.when(exists(oi))
        def _():
            ret_arrival(oi).wait_recv()
    for c in range(BLK):
        total = own_ng[c * BS:(c + 1) * BS, :]
        for oi in range(len(OFFSETS)):
            flags, first, _second = wanted[oi]
            spot = CAP * oi + jnp.where(first == c, 0, 1)
            spot = jnp.where(jnp.logical_and(flags[c], exists(oi)), spot, CAP * len(OFFSETS))
            total = total + ret[spot].astype(F32)
        u = unit[c * BS:(c + 1) * BS, :]
        ug = total * gain_row
        mean = jnp.mean(ug, axis=-1, keepdims=True)
        along = jnp.mean(ug * u, axis=-1, keepdims=True)
        dx[c] = (inv[c * BS:(c + 1) * BS, :] * (ug - mean - u * along)).astype(BF16)

    if fused_sum:
        gather(HEADS - 1)
        gather(HEADS)
        for c in range(HEADS + 1):
            finish(c)
    for oi in range(len(OFFSETS)):
        @pl.when(exists(oi))
        def _():
            halo_copy(oi).wait_send()
            ret_copy(oi).wait_send()


def per_device(n, noise, inputs, norm_gain, qkv_weight, neighbours, out_grad):
    samples, row_count, d = inputs.shape
    hd = d // HEADS
    rows_out = d // n
    grad_scale = 1.0 / math.sqrt(samples * row_count * n * noise)
    fused_sum = n <= 8 and rows_out % 16 == 0 and noise == 2
    vmem = pl.BlockSpec(memory_space=pltpu.VMEM)
    offs = len(OFFSETS)
    scratch = [
        pltpu.VMEM((offs, CAP, BS, d), BF16),
        pltpu.VMEM((offs, CAP, BS, d), BF16),
        pltpu.VMEM((TABLE * BS, d), F32),
        pltpu.VMEM((row_count, 1), F32),
        pltpu.VMEM((d, TABLE * BS), BF16),
        pltpu.VMEM((BLK, BS, d), BF16),
        pltpu.VMEM((TABLE, BS, 2 * d), BF16),
        pltpu.VMEM((row_count, d), BF16),
        pltpu.VMEM((TABLE * BS, 2 * d), BF16),
        pltpu.VMEM((2, BLK * KHOP + 1, BS, 2 * hd), F32),
        pltpu.VMEM((row_count, d), F32),
        pltpu.VMEM((offs, CAP, BS, d), BF16),
        pltpu.VMEM((offs * CAP + 1, BS, d), BF16),
    ] + [pltpu.SemaphoreType.DMA((offs,))] * 4
    out_shape = [jax.ShapeDtypeStruct((BLK, BS, d), BF16)]
    if fused_sum:
        cw = 3 * hd
        scratch += [
            pltpu.VMEM((HEADS, d, cw), BF16),
            pltpu.VMEM((HEADS, d, cw), BF16),
            pltpu.VMEM((HEADS, n, rows_out, cw), BF16),
            pltpu.VMEM((d, BS), BF16),
            pltpu.VMEM((d, BS), BF16),
            pltpu.VMEM((n, rows_out, BS), BF16),
            pltpu.VMEM((HEADS, rows_out, cw), F32),
            pltpu.VMEM((rows_out, BS), F32),
            pltpu.SemaphoreType.DMA((HEADS + 1,)),
            pltpu.SemaphoreType.DMA((HEADS + 1,)),
            pltpu.SemaphoreType.DMA((HEADS + 1, n)),
            pltpu.SemaphoreType.DMA((HEADS + 1, n)),
            pltpu.SemaphoreType.DMA((HEADS + 1,)),
            pltpu.SemaphoreType.DMA((HEADS + 1,)),
        ]
        out_shape += [
            jax.ShapeDtypeStruct((rows_out, 3 * d), F32),
            jax.ShapeDtypeStruct((rows_out, BS), F32),
        ]
    else:
        out_shape += [
            jax.ShapeDtypeStruct((d, 3 * d), F32),
            jax.ShapeDtypeStruct((1, d), F32),
        ]
    dx, w_term, gain_term = pl.pallas_call(
        functools.partial(kernel, n, grad_scale, fused_sum),
        out_shape=out_shape,
        in_specs=[pl.BlockSpec(memory_space=pltpu.SMEM), vmem, vmem, vmem, vmem],
        out_specs=[vmem] * 3,
        scratch_shapes=scratch,
        compiler_params=pltpu.CompilerParams(
            collective_id=0, has_side_effects=True, vmem_limit_bytes=56 * 1024 * 1024
        ),
        cost_estimate=pl.CostEstimate(
            flops=8_000_000_000, bytes_accessed=6_000_000, transcendentals=2_000_000
        ),
    )(
        neighbours,
        inputs.reshape(BLK, BS, d),
        norm_gain.reshape(1, d),
        qkv_weight,
        out_grad.reshape(BLK, BS, d),
    )
    input_grad = dx.reshape(inputs.shape)
    if fused_sum:
        return input_grad, w_term, gain_term[:, 0]
    weight_all = lax.psum(w_term.astype(BF16), "noise").astype(F32)
    gain_all = lax.psum(gain_term[0].astype(BF16), "noise").astype(F32)
    return (
        input_grad,
        lax.psum_scatter(weight_all, "mesh", scatter_dimension=0, tiled=True),
        lax.psum_scatter(gain_all, "mesh", scatter_dimension=0, tiled=True),
    )


def solution(mesh):
    return jax.shard_map(
        functools.partial(per_device, mesh.shape["mesh"], mesh.shape["noise"]),
        mesh=mesh,
        in_specs=(
            P(("groups", "noise"), "mesh", None),
            P(),
            P(),
            P(),
            P(("groups", "noise"), "mesh", None),
        ),
        out_specs=(
            P(("groups", "noise"), "mesh", None),
            P(("groups", "mesh"), None),
            P(("groups", "mesh")),
        ),
        check_vma=False,
    )
```

```python
import functools
import math

import jax
import jax.numpy as jnp
from jax import lax
from jax.experimental import pallas as pl
from jax.experimental.pallas import tpu as pltpu
from jax.sharding import PartitionSpec as P

HEADS = 4
BS = 128
KHOP = 6
BLK = 4
CAP = 2
EPSILON = 1e-05
OFFSETS = (-2, -1, 1, 2)
TABLE = BLK + CAP * len(OFFSETS)
MESH = pl.DeviceIdType.MESH
F32 = jnp.float32
BF16 = jnp.bfloat16


def dot(a, b, dims):
    return lax.dot_general(a, b, (dims, ((), ())), preferred_element_type=F32)


def layer_norm(rows):
    as_float = rows.astype(F32)
    centred = as_float - jnp.mean(as_float, axis=-1, keepdims=True)
    inv_std = lax.rsqrt(jnp.mean(centred * centred, axis=-1, keepdims=True) + EPSILON)
    return centred * inv_std, inv_std


def pick_two(hits):
    first = jnp.int32(BLK - 1)
    for c in reversed(range(BLK - 1)):
        first = jnp.where(hits[c], c, first)
    second = jnp.int32(0)
    for c in reversed(range(1, BLK)):
        second = jnp.where(jnp.logical_and(hits[c], first < c), c, second)
    return first, second


def listed_flags(rows, device):
    flags = []
    for c in range(BLK):
        flag = rows[0] == device * BLK + c
        for entry in rows[1:]:
            flag = jnp.logical_or(flag, entry == device * BLK + c)
        flags.append(flag)
    return flags


def kernel(
    n, grad_scale, fused_sum,
    neigh_any, x_any, gain, w_any, og_any,
    *refs,
):
    outs, scratch = refs[:3], refs[3:]
    dx, w_out, gain_out = outs
    (send, halo, unit, inv, normed_t, q, kv, dq, dkv, terms, own_ng, ret_send, ret,
     halo_ss, halo_rs, ret_ss, ret_rs, neigh, x, w, og, dx_v, in_sem, dx_sem) = scratch[:24]
    loads = [
        pltpu.make_async_copy(src, dst, in_sem.at[i])
        for i, (src, dst) in enumerate(((neigh_any, neigh), (x_any, x), (w_any, w), (og_any, og)))
    ]
    for load in loads:
        load.start()
    me = lax.axis_index("mesh")
    core = lax.axis_index("noise")
    d = x_any.shape[-1]
    hd = d // HEADS
    rows_dev = BLK * BS
    scale = 1.0 / math.sqrt(hd)
    rows_out = d // n
    side = lax.rem(me, 2)
    plane = me // 2
    planes = n // 2
    beside = me + 1 - 2 * side

    def exists(oi):
        other = me + OFFSETS[oi]
        return jnp.logical_and(other >= 0, other < n)

    barrier = pltpu.get_barrier_semaphore()
    if fused_sum:
        for k in range(1, n):
            pl.semaphore_signal(barrier, inc=1, device_id={"mesh": lax.rem(me + k, n)}, device_id_type=MESH)
        pl.semaphore_signal(barrier, inc=1, device_id={"noise": 1 - core}, device_id_type=MESH)
        pl.semaphore_signal(
            barrier, inc=1, device_id={"mesh": beside, "noise": 1 - core}, device_id_type=MESH)
    else:
        for oi in range(len(OFFSETS)):
            @pl.when(exists(oi))
            def _():
                pl.semaphore_signal(barrier, inc=1, device_id={"mesh": me + OFFSETS[oi]}, device_id_type=MESH)

    loads[0].wait()
    loads[1].wait()

    wanted = []
    for oi, off in enumerate(OFFSETS):
        other = jnp.clip(me + off, 0, n - 1)
        entries = [neigh[other * BLK + b, j] for b in range(BLK) for j in range(KHOP)]
        flags = listed_flags(entries, me)
        first, second = pick_two(flags)
        wanted.append((flags, first, second))
        send[oi, 0] = x[first]
        send[oi, 1] = x[second]

    if fused_sum:
        pl.semaphore_wait(barrier, n + 1)
    else:
        for oi in range(len(OFFSETS)):
            @pl.when(exists(oi))
            def _():
                pl.semaphore_wait(barrier, 1)

    def halo_copy(oi):
        return pltpu.make_async_remote_copy(
            src_ref=send.at[oi], dst_ref=halo.at[3 - oi],
            send_sem=halo_ss.at[oi], recv_sem=halo_rs.at[3 - oi],
            device_id={"mesh": me + OFFSETS[oi]}, device_id_type=MESH)

    def halo_arrival(oi):
        return pltpu.make_async_remote_copy(
            src_ref=send.at[oi], dst_ref=halo.at[oi],
            send_sem=halo_ss.at[oi], recv_sem=halo_rs.at[oi],
            device_id={"mesh": me + OFFSETS[oi]}, device_id_type=MESH)

    for oi in (0, 3, 1, 2):
        @pl.when(exists(oi))
        def _():
            halo_copy(oi).start()

        @pl.when(jnp.logical_not(exists(oi)))
        def _():
            halo[oi] = jnp.zeros(halo.shape[1:], BF16)

    mine = [[neigh[me * BLK + b, j] for j in range(KHOP)] for b in range(BLK)]
    flat = [entry for row in mine for entry in row]
    table_id = [me * BLK + c for c in range(BLK)]
    for oi, off in enumerate(OFFSETS):
        flags = listed_flags(flat, me + off)
        first, second = pick_two(flags)
        base = (me + off) * BLK
        table_id.append(jnp.where(functools.reduce(jnp.logical_or, flags), base + first, -1))
        table_id.append(jnp.where(second > 0, base + second, -1))
    where_from = [[None] * KHOP for _ in range(BLK)]
    back = [[None] * BLK for _ in range(TABLE)]
    none = BLK * KHOP
    for b in range(BLK):
        spots = [jnp.int32(0)] * KHOP
        for t in range(TABLE):
            found = jnp.int32(none)
            for j in range(KHOP):
                same = mine[b][j] == table_id[t]
                spots[j] = jnp.where(same, t, spots[j])
                found = jnp.where(same, b * KHOP + j, found)
            back[t][b] = found
        where_from[b] = spots

    gain_row = gain[...]

    u, istd = layer_norm(x[...].reshape(rows_dev, d))
    unit[:rows_dev, :] = u
    inv[...] = istd
    normed = (u * gain_row).astype(BF16)
    loads[2].wait()
    q[...] = dot(normed, w[:, :d], ((1,), (0,))).astype(BF16).reshape(BLK, BS, d)
    kv[:BLK] = dot(normed, w[:, d:], ((1,), (0,))).astype(BF16).reshape(BLK, BS, 2 * d)
    normed_t[:, :rows_dev] = normed.T
    loads[3].wait()
    for s in range(2):
        terms[s, none] = jnp.zeros(terms.shape[2:], F32)
    ret[CAP * len(OFFSETS)] = jnp.zeros(ret.shape[1:], BF16)

    for oi in (0, 3, 1, 2):
        @pl.when(exists(oi))
        def _():
            halo_arrival(oi).wait_recv()
        t = BLK + CAP * oi
        u, _istd = layer_norm(halo[oi].reshape(CAP * BS, d))
        unit[t * BS:(t + CAP) * BS, :] = u
        normed = (u * gain_row).astype(BF16)
        kv[t:t + CAP] = dot(normed, w[:, d:], ((1,), (0,))).astype(BF16).reshape(CAP, BS, 2 * d)
        normed_t[:, t * BS:(t + CAP) * BS] = normed.T

    if fused_sum:
        (chunk, quad, held, parts, gchunk, gquad, gheld, gparts, done, gdone,
         quad_ss, quad_rs, part_ss, part_rs, done_ss, done_rs) = scratch[24:]

        def bufs(c):
            if c < HEADS:
                return chunk.at[c], quad.at[c], held.at[c], parts.at[c], done.at[c]
            return gchunk, gquad, gheld, gparts, gdone

        def quad_copy(c, to_side, device, place):
            return pltpu.make_async_remote_copy(
                src_ref=bufs(c)[0].at[to_side], dst_ref=bufs(c)[1].at[place],
                send_sem=quad_ss.at[c, place], recv_sem=quad_rs.at[c, place],
                device_id=device, device_id_type=MESH)

        def from_sibling(c):
            return quad_copy(c, side, {"noise": 1 - core}, 0)

        def from_beside(c):
            return quad_copy(c, 1 - side, {"mesh": beside}, 1)

        def from_across(c):
            return quad_copy(c, 1 - side, {"mesh": beside, "noise": 1 - core}, 2)

        def to_plane(c, k):
            _chunk, _quad, held_c, parts_c, _done = bufs(c)
            return pltpu.make_async_remote_copy(
                src_ref=held_c.at[lax.rem(plane + k, planes)],
                dst_ref=parts_c.at[k], send_sem=part_ss.at[c, k], recv_sem=part_rs.at[c, k],
                device_id={"mesh": lax.rem(me + 2 * k, n)}, device_id_type=MESH)

        def final_copy(c):
            done_c = bufs(c)[4]
            return pltpu.make_async_remote_copy(
                src_ref=done_c, dst_ref=done_c, send_sem=done_ss.at[c], recv_sem=done_rs.at[c],
                device_id={"noise": 1 - core}, device_id_type=MESH)

        def begin(c):
            @pl.when(core != c % 2)
            def _():
                from_across(c).start()
                from_sibling(c).start()

            @pl.when(core == c % 2)
            def _():
                from_beside(c).start()

        def spread(c):
            @pl.when(core == c % 2)
            def _():
                chunk_c, quad_c, held_c, _parts, _done = bufs(c)
                from_sibling(c).wait_recv()
                from_beside(c).wait_recv()
                from_across(c).wait_recv()
                total = chunk_c[side].astype(F32)
                for place in range(3):
                    total = total + quad_c[place].astype(F32)
                held_c[...] = total.astype(BF16)
                for k in range(1, planes):
                    to_plane(c, k).start()

        def gather(c):
            @pl.when(core == c % 2)
            def _():
                _chunk, _quad, held_c, parts_c, done_c = bufs(c)
                total = held_c[plane].astype(F32)
                for k in range(1, planes):
                    to_plane(c, k).wait_recv()
                    total = total + parts_c[k].astype(F32)
                done_c[...] = total
                final_copy(c).start()

        def finish(c):
            @pl.when(core == c % 2)
            def _():
                final_copy(c).wait_send()
                from_beside(c).wait_send()
                for k in range(1, planes):
                    to_plane(c, k).wait_send()

            @pl.when(core != c % 2)
            def _():
                from_across(c).wait_send()
                from_sibling(c).wait_send()
                final_copy(c).wait_recv()
            done_c = bufs(c)[4]
            if c < HEADS:
                for part in range(3):
                    w_out[:, part * d + c * hd:part * d + (c + 1) * hd] = done_c[:, part * hd:(part + 1) * hd]
            else:
                gain_out[...] = done_c[...]

    def weight_product(h):
        lo, hi = h * hd, (h + 1) * hd
        wq = dot(normed_t[:, :rows_dev], dq[:, lo:hi], ((1,), (0,))) * grad_scale
        kv_cols = jnp.concatenate([dkv[:, lo:hi], dkv[:, d + lo:d + hi]], axis=1)
        wkv = dot(normed_t[...], kv_cols, ((1,), (0,))) * grad_scale
        if fused_sum:
            wq, wkv = wq.astype(BF16), wkv.astype(BF16)
            for p in range(n):
                rows = slice(p * rows_out, (p + 1) * rows_out)
                chunk[h, p % 2, p // 2, :, :hd] = wq[rows]
                chunk[h, p % 2, p // 2, :, hd:] = wkv[rows]
            begin(h)
        else:
            w_out[:, lo:hi] = wq
            w_out[:, d + lo:d + hi] = wkv[:, :hd]
            w_out[:, 2 * d + lo:2 * d + hi] = wkv[:, hd:]

    for h in range(HEADS):
        lo, hi = h * hd, (h + 1) * hd
        buf = h % 2
        for b in range(BLK):
            kg = jnp.concatenate([kv[where_from[b][j], :, lo:hi] for j in range(KHOP)], axis=0)
            vg = jnp.concatenate([kv[where_from[b][j], :, d + lo:d + hi] for j in range(KHOP)], axis=0)
            qh = q[b, :, lo:hi]
            gh = og[b, :, lo:hi]
            s = dot(kg, qh, ((1,), (1,)))
            top = jnp.max(s, axis=0, keepdims=True)
            p = jnp.exp2((s - top) * (scale * math.log2(math.e)))
            a = p * (1.0 / jnp.sum(p, axis=0, keepdims=True))
            a_low = a.astype(BF16)
            da = dot(vg, gh, ((1,), (1,)))
            row_dot = jnp.sum(a_low.astype(F32) * da, axis=0, keepdims=True)
            ds = (a * (da - row_dot)).astype(BF16)
            dq[b * BS:(b + 1) * BS, lo:hi] = (dot(ds, kg, ((0,), (0,))) * scale).astype(BF16)
            dk = dot(ds, qh, ((1,), (0,))) * scale
            dv = dot(a_low, gh, ((1,), (0,)))
            for j in range(KHOP):
                terms[buf, b * KHOP + j, :, :hd] = dk[j * BS:(j + 1) * BS]
                terms[buf, b * KHOP + j, :, hd:] = dv[j * BS:(j + 1) * BS]
        for t in range(TABLE):
            total = terms[buf, back[t][0]]
            for b in range(1, BLK):
                total = total + terms[buf, back[t][b]]
            dkv[t * BS:(t + 1) * BS, lo:hi] = total[:, :hd].astype(BF16)
            dkv[t * BS:(t + 1) * BS, d + lo:d + hi] = total[:, hd:].astype(BF16)
        if h < HEADS - 1:
            weight_product(h)
        if fused_sum and h >= 1:
            spread(h - 1)

    def ret_copy(oi):
        return pltpu.make_async_remote_copy(
            src_ref=ret_send.at[oi], dst_ref=ret.at[pl.ds(CAP * (3 - oi), CAP)],
            send_sem=ret_ss.at[oi], recv_sem=ret_rs.at[3 - oi],
            device_id={"mesh": me + OFFSETS[oi]}, device_id_type=MESH)

    def ret_arrival(oi):
        return pltpu.make_async_remote_copy(
            src_ref=ret_send.at[oi], dst_ref=ret.at[pl.ds(CAP * oi, CAP)],
            send_sem=ret_ss.at[oi], recv_sem=ret_rs.at[oi],
            device_id={"mesh": me + OFFSETS[oi]}, device_id_type=MESH)

    gain_sum = jnp.zeros((1, d), F32)
    for oi in (0, 3, 1, 2):
        r0 = (BLK + CAP * oi) * BS
        ng = dot(dkv[r0:r0 + CAP * BS, :], w[:, d:], ((1,), (1,)))
        gain_sum += jnp.sum(ng * unit[r0:r0 + CAP * BS, :], axis=0, keepdims=True)
        for slot in range(CAP):
            ret_send[oi, slot] = ng[slot * BS:(slot + 1) * BS].astype(BF16)

        @pl.when(exists(oi))
        def _():
            ret_copy(oi).start()
    weight_product(HEADS - 1)
    ng = dot(dq[...], w[:, :d], ((1,), (1,))) + dot(dkv[:rows_dev, :], w[:, d:], ((1,), (1,)))
    own_ng[...] = ng
    gain_sum += jnp.sum(ng * unit[:rows_dev, :], axis=0, keepdims=True)
    gain_sum = gain_sum * grad_scale
    if fused_sum:
        column = jnp.broadcast_to(gain_sum, (BS, d)).T.astype(BF16)
        for p in range(n):
            gchunk[p % 2, p // 2] = column[p * rows_out:(p + 1) * rows_out]
        begin(HEADS)
        for c in range(HEADS - 2):
            gather(c)
        spread(HEADS - 1)
        gather(HEADS - 2)
        spread(HEADS)
    else:
        gain_out[...] = gain_sum

    for oi in range(len(OFFSETS)):
        @pl.when(exists(oi))
        def _():
            ret_arrival(oi).wait_recv()
    for c in range(BLK):
        total = own_ng[c * BS:(c + 1) * BS, :]
        for oi in range(len(OFFSETS)):
            flags, first, _second = wanted[oi]
            spot = CAP * oi + jnp.where(first == c, 0, 1)
            spot = jnp.where(jnp.logical_and(flags[c], exists(oi)), spot, CAP * len(OFFSETS))
            total = total + ret[spot].astype(F32)
        u = unit[c * BS:(c + 1) * BS, :]
        ug = total * gain_row
        mean = jnp.mean(ug, axis=-1, keepdims=True)
        along = jnp.mean(ug * u, axis=-1, keepdims=True)
        dx_v[c] = (inv[c * BS:(c + 1) * BS, :] * (ug - mean - u * along)).astype(BF16)

    dx_copy = pltpu.make_async_copy(dx_v, dx, dx_sem)
    dx_copy.start()
    if fused_sum:
        gather(HEADS - 1)
        gather(HEADS)
        for c in range(HEADS + 1):
            finish(c)
    for oi in range(len(OFFSETS)):
        @pl.when(exists(oi))
        def _():
            halo_copy(oi).wait_send()
            ret_copy(oi).wait_send()
    dx_copy.wait()


def per_device(n, noise, inputs, norm_gain, qkv_weight, neighbours, out_grad):
    samples, row_count, d = inputs.shape
    hd = d // HEADS
    rows_out = d // n
    grad_scale = 1.0 / math.sqrt(samples * row_count * n * noise)
    fused_sum = n <= 8 and n % 2 == 0 and rows_out % 16 == 0 and noise == 2
    vmem = pl.BlockSpec(memory_space=pltpu.VMEM)
    anywhere = pl.BlockSpec(memory_space=pl.ANY)
    offs = len(OFFSETS)
    scratch = [
        pltpu.VMEM((offs, CAP, BS, d), BF16),
        pltpu.VMEM((offs, CAP, BS, d), BF16),
        pltpu.VMEM((TABLE * BS, d), F32),
        pltpu.VMEM((row_count, 1), F32),
        pltpu.VMEM((d, TABLE * BS), BF16),
        pltpu.VMEM((BLK, BS, d), BF16),
        pltpu.VMEM((TABLE, BS, 2 * d), BF16),
        pltpu.VMEM((row_count, d), BF16),
        pltpu.VMEM((TABLE * BS, 2 * d), BF16),
        pltpu.VMEM((2, BLK * KHOP + 1, BS, 2 * hd), F32),
        pltpu.VMEM((row_count, d), F32),
        pltpu.VMEM((offs, CAP, BS, d), BF16),
        pltpu.VMEM((offs * CAP + 1, BS, d), BF16),
    ] + [pltpu.SemaphoreType.DMA((offs,))] * 4 + [
        pltpu.SMEM(neighbours.shape, jnp.int32),
        pltpu.VMEM((BLK, BS, d), BF16),
        pltpu.VMEM((d, 3 * d), BF16),
        pltpu.VMEM((BLK, BS, d), BF16),
        pltpu.VMEM((BLK, BS, d), BF16),
        pltpu.SemaphoreType.DMA((4,)),
        pltpu.SemaphoreType.DMA,
    ]
    out_shape = [jax.ShapeDtypeStruct((BLK, BS, d), BF16)]
    if fused_sum:
        cw = 3 * hd
        scratch += [
            pltpu.VMEM((HEADS, 2, n // 2, rows_out, cw), BF16),
            pltpu.VMEM((HEADS, 3, n // 2, rows_out, cw), BF16),
            pltpu.VMEM((HEADS, n // 2, rows_out, cw), BF16),
            pltpu.VMEM((HEADS, n // 2, rows_out, cw), BF16),
            pltpu.VMEM((2, n // 2, rows_out, BS), BF16),
            pltpu.VMEM((3, n // 2, rows_out, BS), BF16),
            pltpu.VMEM((n // 2, rows_out, BS), BF16),
            pltpu.VMEM((n // 2, rows_out, BS), BF16),
            pltpu.VMEM((HEADS, rows_out, cw), F32),
            pltpu.VMEM((rows_out, BS), F32),
            pltpu.SemaphoreType.DMA((HEADS + 1, 3)),
            pltpu.SemaphoreType.DMA((HEADS + 1, 3)),
            pltpu.SemaphoreType.DMA((HEADS + 1, n // 2)),
            pltpu.SemaphoreType.DMA((HEADS + 1, n // 2)),
            pltpu.SemaphoreType.DMA((HEADS + 1,)),
            pltpu.SemaphoreType.DMA((HEADS + 1,)),
        ]
        out_shape += [
            jax.ShapeDtypeStruct((rows_out, 3 * d), F32),
            jax.ShapeDtypeStruct((rows_out, BS), F32),
        ]
    else:
        out_shape += [
            jax.ShapeDtypeStruct((d, 3 * d), F32),
            jax.ShapeDtypeStruct((1, d), F32),
        ]
    dx, w_term, gain_term = pl.pallas_call(
        functools.partial(kernel, n, grad_scale, fused_sum),
        out_shape=out_shape,
        in_specs=[anywhere, anywhere, vmem, anywhere, anywhere],
        out_specs=[anywhere, vmem, vmem],
        scratch_shapes=scratch,
        compiler_params=pltpu.CompilerParams(
            collective_id=0, has_side_effects=True, vmem_limit_bytes=56 * 1024 * 1024
        ),
        cost_estimate=pl.CostEstimate(
            flops=8_000_000_000, bytes_accessed=6_000_000, transcendentals=2_000_000
        ),
    )(
        neighbours,
        inputs.reshape(BLK, BS, d),
        norm_gain.reshape(1, d),
        qkv_weight,
        out_grad.reshape(BLK, BS, d),
    )
    input_grad = dx.reshape(inputs.shape)
    if fused_sum:
        return input_grad, w_term, gain_term[:, 0]
    weight_all = lax.psum(w_term.astype(BF16), "noise").astype(F32)
    gain_all = lax.psum(gain_term[0].astype(BF16), "noise").astype(F32)
    return (
        input_grad,
        lax.psum_scatter(weight_all, "mesh", scatter_dimension=0, tiled=True),
        lax.psum_scatter(gain_all, "mesh", scatter_dimension=0, tiled=True),
    )


def solution(mesh):
    return jax.shard_map(
        functools.partial(per_device, mesh.shape["mesh"], mesh.shape["noise"]),
        mesh=mesh,
        in_specs=(
            P(("groups", "noise"), "mesh", None),
            P(),
            P(),
            P(),
            P(("groups", "noise"), "mesh", None),
        ),
        out_specs=(
            P(("groups", "noise"), "mesh", None),
            P(("groups", "mesh"), None),
            P(("groups", "mesh")),
        ),
        check_vma=False,
    )
```

```python
import functools
import math

import jax
import jax.numpy as jnp
from jax import lax
from jax.experimental import pallas as pl
from jax.experimental.pallas import tpu as pltpu
from jax.sharding import PartitionSpec as P

HEADS = 4
BS = 128
KHOP = 6
BLK = 4
CAP = 2
EPSILON = 1e-05
OFFSETS = (-2, -1, 1, 2)
TABLE = BLK + CAP * len(OFFSETS)
MESH = pl.DeviceIdType.MESH
F32 = jnp.float32
BF16 = jnp.bfloat16


def dot(a, b, dims):
    return lax.dot_general(a, b, (dims, ((), ())), preferred_element_type=F32)


def layer_norm(rows):
    as_float = rows.astype(F32)
    centred = as_float - jnp.mean(as_float, axis=-1, keepdims=True)
    inv_std = lax.rsqrt(jnp.mean(centred * centred, axis=-1, keepdims=True) + EPSILON)
    return centred * inv_std, inv_std


def pick_two(hits):
    first = jnp.int32(BLK - 1)
    for c in reversed(range(BLK - 1)):
        first = jnp.where(hits[c], c, first)
    second = jnp.int32(0)
    for c in reversed(range(1, BLK)):
        second = jnp.where(jnp.logical_and(hits[c], first < c), c, second)
    return first, second


def listed_flags(rows, device):
    flags = []
    for c in range(BLK):
        flag = rows[0] == device * BLK + c
        for entry in rows[1:]:
            flag = jnp.logical_or(flag, entry == device * BLK + c)
        flags.append(flag)
    return flags


def kernel(
    n, grad_scale, fused_sum,
    neigh_any, x_any, gain, w_any, og_any,
    *refs,
):
    outs, scratch = refs[:3], refs[3:]
    dx, w_out, gain_out = outs
    (send, halo, unit, inv, normed_t, q, kv, dq, dkv, terms, own_ng, ret_send, ret,
     halo_ss, halo_rs, ret_ss, ret_rs, neigh, x, w, og, dx_v, in_sem, dx_sem) = scratch[:24]
    loads = [
        pltpu.make_async_copy(src, dst, in_sem.at[i])
        for i, (src, dst) in enumerate(((neigh_any, neigh), (x_any, x), (w_any, w), (og_any, og)))
    ]
    for load in loads:
        load.start()
    me = lax.axis_index("mesh")
    core = lax.axis_index("noise")
    d = x_any.shape[-1]
    hd = d // HEADS
    rows_dev = BLK * BS
    scale = 1.0 / math.sqrt(hd)
    rows_out = d // n
    side = lax.rem(me, 2)
    plane = me // 2
    planes = n // 2
    beside = me + 1 - 2 * side

    def exists(oi):
        other = me + OFFSETS[oi]
        return jnp.logical_and(other >= 0, other < n)

    barrier = pltpu.get_barrier_semaphore()
    if fused_sum:
        for k in range(1, n):
            pl.semaphore_signal(barrier, inc=1, device_id={"mesh": lax.rem(me + k, n)}, device_id_type=MESH)
        pl.semaphore_signal(barrier, inc=1, device_id={"noise": 1 - core}, device_id_type=MESH)
        pl.semaphore_signal(
            barrier, inc=1, device_id={"mesh": beside, "noise": 1 - core}, device_id_type=MESH)
    else:
        for oi in range(len(OFFSETS)):
            @pl.when(exists(oi))
            def _():
                pl.semaphore_signal(barrier, inc=1, device_id={"mesh": me + OFFSETS[oi]}, device_id_type=MESH)

    loads[0].wait()
    loads[1].wait()

    wanted = []
    for oi, off in enumerate(OFFSETS):
        other = jnp.clip(me + off, 0, n - 1)
        entries = [neigh[other * BLK + b, j] for b in range(BLK) for j in range(KHOP)]
        flags = listed_flags(entries, me)
        first, second = pick_two(flags)
        wanted.append((flags, first, second))
        send[oi, 0] = x[first]
        send[oi, 1] = x[second]

    if fused_sum:
        pl.semaphore_wait(barrier, n + 1)
    else:
        for oi in range(len(OFFSETS)):
            @pl.when(exists(oi))
            def _():
                pl.semaphore_wait(barrier, 1)

    def halo_copy(oi):
        return pltpu.make_async_remote_copy(
            src_ref=send.at[oi], dst_ref=halo.at[3 - oi],
            send_sem=halo_ss.at[oi], recv_sem=halo_rs.at[3 - oi],
            device_id={"mesh": me + OFFSETS[oi]}, device_id_type=MESH)

    def halo_arrival(oi):
        return pltpu.make_async_remote_copy(
            src_ref=send.at[oi], dst_ref=halo.at[oi],
            send_sem=halo_ss.at[oi], recv_sem=halo_rs.at[oi],
            device_id={"mesh": me + OFFSETS[oi]}, device_id_type=MESH)

    for oi in (0, 3, 1, 2):
        @pl.when(exists(oi))
        def _():
            halo_copy(oi).start()

        @pl.when(jnp.logical_not(exists(oi)))
        def _():
            halo[oi] = jnp.zeros(halo.shape[1:], BF16)

    mine = [[neigh[me * BLK + b, j] for j in range(KHOP)] for b in range(BLK)]
    flat = [entry for row in mine for entry in row]
    table_id = [me * BLK + c for c in range(BLK)]
    for oi, off in enumerate(OFFSETS):
        flags = listed_flags(flat, me + off)
        first, second = pick_two(flags)
        base = (me + off) * BLK
        table_id.append(jnp.where(functools.reduce(jnp.logical_or, flags), base + first, -1))
        table_id.append(jnp.where(second > 0, base + second, -1))
    where_from = [[None] * KHOP for _ in range(BLK)]
    back = [[None] * BLK for _ in range(TABLE)]
    none = BLK * KHOP
    for b in range(BLK):
        spots = [jnp.int32(0)] * KHOP
        for t in range(TABLE):
            found = jnp.int32(none)
            for j in range(KHOP):
                same = mine[b][j] == table_id[t]
                spots[j] = jnp.where(same, t, spots[j])
                found = jnp.where(same, b * KHOP + j, found)
            back[t][b] = found
        where_from[b] = spots

    gain_row = gain[...]

    u, istd = layer_norm(x[...].reshape(rows_dev, d))
    unit[:rows_dev, :] = u
    inv[...] = istd
    normed = (u * gain_row).astype(BF16)
    loads[2].wait()
    q[...] = dot(normed, w[:, :d], ((1,), (0,))).astype(BF16).reshape(BLK, BS, d)
    kv[:BLK] = dot(normed, w[:, d:], ((1,), (0,))).astype(BF16).reshape(BLK, BS, 2 * d)
    normed_t[:, :rows_dev] = normed.T
    loads[3].wait()
    for s in range(2):
        terms[s, none] = jnp.zeros(terms.shape[2:], F32)
    ret[CAP * len(OFFSETS)] = jnp.zeros(ret.shape[1:], BF16)

    for oi in (0, 3, 1, 2):
        @pl.when(exists(oi))
        def _():
            halo_arrival(oi).wait_recv()
        t = BLK + CAP * oi
        u, _istd = layer_norm(halo[oi].reshape(CAP * BS, d))
        unit[t * BS:(t + CAP) * BS, :] = u
        normed = (u * gain_row).astype(BF16)
        kv[t:t + CAP] = dot(normed, w[:, d:], ((1,), (0,))).astype(BF16).reshape(CAP, BS, 2 * d)
        normed_t[:, t * BS:(t + CAP) * BS] = normed.T

    if fused_sum:
        (chunk, quad, held, parts, gchunk, gquad, gheld, gparts, done, gdone,
         quad_ss, quad_rs, part_ss, part_rs, done_ss, done_rs) = scratch[24:]

        def bufs(c):
            if c < HEADS:
                return chunk.at[c], quad.at[c], held.at[c], parts.at[c], done.at[c]
            return gchunk, gquad, gheld, gparts, gdone

        def quad_copy(c, to_side, device, place):
            return pltpu.make_async_remote_copy(
                src_ref=bufs(c)[0].at[to_side], dst_ref=bufs(c)[1].at[place],
                send_sem=quad_ss.at[c, place], recv_sem=quad_rs.at[c, place],
                device_id=device, device_id_type=MESH)

        def from_sibling(c):
            return quad_copy(c, side, {"noise": 1 - core}, 0)

        def from_beside(c):
            return quad_copy(c, 1 - side, {"mesh": beside}, 1)

        def from_across(c):
            return quad_copy(c, 1 - side, {"mesh": beside, "noise": 1 - core}, 2)

        def to_plane(c, k):
            _chunk, _quad, held_c, parts_c, _done = bufs(c)
            return pltpu.make_async_remote_copy(
                src_ref=held_c.at[lax.rem(plane + k, planes)],
                dst_ref=parts_c.at[k], send_sem=part_ss.at[c, k], recv_sem=part_rs.at[c, k],
                device_id={"mesh": lax.rem(me + 2 * k, n)}, device_id_type=MESH)

        def final_copy(c):
            done_c = bufs(c)[4]
            return pltpu.make_async_remote_copy(
                src_ref=done_c, dst_ref=done_c, send_sem=done_ss.at[c], recv_sem=done_rs.at[c],
                device_id={"noise": 1 - core}, device_id_type=MESH)

        def begin(c):
            @pl.when(core != c % 2)
            def _():
                from_across(c).start()
                from_sibling(c).start()

            @pl.when(core == c % 2)
            def _():
                from_beside(c).start()

        def spread(c):
            @pl.when(core == c % 2)
            def _():
                chunk_c, quad_c, held_c, _parts, _done = bufs(c)
                from_sibling(c).wait_recv()
                from_beside(c).wait_recv()
                from_across(c).wait_recv()
                total = chunk_c[side].astype(F32)
                for place in range(3):
                    total = total + quad_c[place].astype(F32)
                held_c[...] = total.astype(BF16)
                for k in range(1, planes):
                    to_plane(c, k).start()

        def gather(c):
            @pl.when(core == c % 2)
            def _():
                _chunk, _quad, held_c, parts_c, done_c = bufs(c)
                total = held_c[plane].astype(F32)
                for k in range(1, planes):
                    to_plane(c, k).wait_recv()
                    total = total + parts_c[k].astype(F32)
                done_c[...] = total
                final_copy(c).start()

        def finish(c):
            @pl.when(core == c % 2)
            def _():
                final_copy(c).wait_send()
                from_beside(c).wait_send()
                for k in range(1, planes):
                    to_plane(c, k).wait_send()

            @pl.when(core != c % 2)
            def _():
                from_across(c).wait_send()
                from_sibling(c).wait_send()
                final_copy(c).wait_recv()
            done_c = bufs(c)[4]
            if c < HEADS:
                for part in range(3):
                    w_out[:, part * d + c * hd:part * d + (c + 1) * hd] = done_c[:, part * hd:(part + 1) * hd]
            else:
                gain_out[...] = done_c[...]

    def weight_product(h):
        lo, hi = h * hd, (h + 1) * hd
        wq = dot(normed_t[:, :rows_dev], dq[:, lo:hi], ((1,), (0,))) * grad_scale
        kv_cols = jnp.concatenate([dkv[:, lo:hi], dkv[:, d + lo:d + hi]], axis=1)
        wkv = dot(normed_t[...], kv_cols, ((1,), (0,))) * grad_scale
        if fused_sum:
            wq, wkv = wq.astype(BF16), wkv.astype(BF16)
            for p in range(n):
                rows = slice(p * rows_out, (p + 1) * rows_out)
                chunk[h, p % 2, p // 2, :, :hd] = wq[rows]
                chunk[h, p % 2, p // 2, :, hd:] = wkv[rows]
            begin(h)
        else:
            w_out[:, lo:hi] = wq
            w_out[:, d + lo:d + hi] = wkv[:, :hd]
            w_out[:, 2 * d + lo:2 * d + hi] = wkv[:, hd:]

    for h in range(HEADS):
        lo, hi = h * hd, (h + 1) * hd
        buf = h % 2
        for b in range(BLK):
            kg = jnp.concatenate([kv[where_from[b][j], :, lo:hi] for j in range(KHOP)], axis=0)
            vg = jnp.concatenate([kv[where_from[b][j], :, d + lo:d + hi] for j in range(KHOP)], axis=0)
            qh = q[b, :, lo:hi]
            gh = og[b, :, lo:hi]
            s = dot(kg, qh, ((1,), (1,)))
            top = jnp.max(s, axis=0, keepdims=True)
            p = jnp.exp2((s - top) * (scale * math.log2(math.e)))
            a = p * (1.0 / jnp.sum(p, axis=0, keepdims=True))
            a_low = a.astype(BF16)
            da = dot(vg, gh, ((1,), (1,)))
            row_dot = jnp.sum(a_low.astype(F32) * da, axis=0, keepdims=True)
            ds = (a * (da - row_dot)).astype(BF16)
            dq[b * BS:(b + 1) * BS, lo:hi] = (dot(ds, kg, ((0,), (0,))) * scale).astype(BF16)
            dk = dot(ds, qh, ((1,), (0,))) * scale
            dv = dot(a_low, gh, ((1,), (0,)))
            for j in range(KHOP):
                terms[buf, b * KHOP + j, :, :hd] = dk[j * BS:(j + 1) * BS]
                terms[buf, b * KHOP + j, :, hd:] = dv[j * BS:(j + 1) * BS]
        for t in range(TABLE):
            total = terms[buf, back[t][0]]
            for b in range(1, BLK):
                total = total + terms[buf, back[t][b]]
            dkv[t * BS:(t + 1) * BS, lo:hi] = total[:, :hd].astype(BF16)
            dkv[t * BS:(t + 1) * BS, d + lo:d + hi] = total[:, hd:].astype(BF16)
        weight_product(h)
        if fused_sum and h >= 1:
            spread(h - 1)

    def ret_copy(oi):
        return pltpu.make_async_remote_copy(
            src_ref=ret_send.at[oi], dst_ref=ret.at[pl.ds(CAP * (3 - oi), CAP)],
            send_sem=ret_ss.at[oi], recv_sem=ret_rs.at[3 - oi],
            device_id={"mesh": me + OFFSETS[oi]}, device_id_type=MESH)

    def ret_arrival(oi):
        return pltpu.make_async_remote_copy(
            src_ref=ret_send.at[oi], dst_ref=ret.at[pl.ds(CAP * oi, CAP)],
            send_sem=ret_ss.at[oi], recv_sem=ret_rs.at[oi],
            device_id={"mesh": me + OFFSETS[oi]}, device_id_type=MESH)

    gain_sum = jnp.zeros((1, d), F32)
    for oi in (0, 3, 1, 2):
        r0 = (BLK + CAP * oi) * BS
        ng = dot(dkv[r0:r0 + CAP * BS, :], w[:, d:], ((1,), (1,)))
        gain_sum += jnp.sum(ng * unit[r0:r0 + CAP * BS, :], axis=0, keepdims=True)
        for slot in range(CAP):
            ret_send[oi, slot] = ng[slot * BS:(slot + 1) * BS].astype(BF16)

        @pl.when(exists(oi))
        def _():
            ret_copy(oi).start()
    ng = dot(dq[...], w[:, :d], ((1,), (1,))) + dot(dkv[:rows_dev, :], w[:, d:], ((1,), (1,)))
    own_ng[...] = ng
    gain_sum += jnp.sum(ng * unit[:rows_dev, :], axis=0, keepdims=True)
    gain_sum = gain_sum * grad_scale
    if fused_sum:
        column = jnp.broadcast_to(gain_sum, (BS, d)).T.astype(BF16)
        for p in range(n):
            gchunk[p % 2, p // 2] = column[p * rows_out:(p + 1) * rows_out]
        begin(HEADS)
        spread(HEADS - 1)
        for c in range(HEADS - 1):
            gather(c)
        spread(HEADS)
        for c in range(HEADS - 1):
            finish(c)
    else:
        gain_out[...] = gain_sum

    for oi in range(len(OFFSETS)):
        @pl.when(exists(oi))
        def _():
            ret_arrival(oi).wait_recv()
    for c in range(BLK):
        total = own_ng[c * BS:(c + 1) * BS, :]
        for oi in range(len(OFFSETS)):
            flags, first, _second = wanted[oi]
            spot = CAP * oi + jnp.where(first == c, 0, 1)
            spot = jnp.where(jnp.logical_and(flags[c], exists(oi)), spot, CAP * len(OFFSETS))
            total = total + ret[spot].astype(F32)
        u = unit[c * BS:(c + 1) * BS, :]
        ug = total * gain_row
        mean = jnp.mean(ug, axis=-1, keepdims=True)
        along = jnp.mean(ug * u, axis=-1, keepdims=True)
        dx_v[c] = (inv[c * BS:(c + 1) * BS, :] * (ug - mean - u * along)).astype(BF16)

    dx_copy = pltpu.make_async_copy(dx_v, dx, dx_sem)
    dx_copy.start()
    if fused_sum:
        gather(HEADS - 1)
        gather(HEADS)
        for c in (HEADS - 1, HEADS):
            finish(c)
    for oi in range(len(OFFSETS)):
        @pl.when(exists(oi))
        def _():
            halo_copy(oi).wait_send()
            ret_copy(oi).wait_send()
    dx_copy.wait()


def per_device(n, noise, inputs, norm_gain, qkv_weight, neighbours, out_grad):
    samples, row_count, d = inputs.shape
    hd = d // HEADS
    rows_out = d // n
    grad_scale = 1.0 / math.sqrt(samples * row_count * n * noise)
    fused_sum = n <= 8 and n % 2 == 0 and rows_out % 16 == 0 and noise == 2
    vmem = pl.BlockSpec(memory_space=pltpu.VMEM)
    anywhere = pl.BlockSpec(memory_space=pl.ANY)
    offs = len(OFFSETS)
    scratch = [
        pltpu.VMEM((offs, CAP, BS, d), BF16),
        pltpu.VMEM((offs, CAP, BS, d), BF16),
        pltpu.VMEM((TABLE * BS, d), F32),
        pltpu.VMEM((row_count, 1), F32),
        pltpu.VMEM((d, TABLE * BS), BF16),
        pltpu.VMEM((BLK, BS, d), BF16),
        pltpu.VMEM((TABLE, BS, 2 * d), BF16),
        pltpu.VMEM((row_count, d), BF16),
        pltpu.VMEM((TABLE * BS, 2 * d), BF16),
        pltpu.VMEM((2, BLK * KHOP + 1, BS, 2 * hd), F32),
        pltpu.VMEM((row_count, d), F32),
        pltpu.VMEM((offs, CAP, BS, d), BF16),
        pltpu.VMEM((offs * CAP + 1, BS, d), BF16),
    ] + [pltpu.SemaphoreType.DMA((offs,))] * 4 + [
        pltpu.SMEM(neighbours.shape, jnp.int32),
        pltpu.VMEM((BLK, BS, d), BF16),
        pltpu.VMEM((d, 3 * d), BF16),
        pltpu.VMEM((BLK, BS, d), BF16),
        pltpu.VMEM((BLK, BS, d), BF16),
        pltpu.SemaphoreType.DMA((4,)),
        pltpu.SemaphoreType.DMA,
    ]
    out_shape = [jax.ShapeDtypeStruct((BLK, BS, d), BF16)]
    if fused_sum:
        cw = 3 * hd
        scratch += [
            pltpu.VMEM((HEADS, 2, n // 2, rows_out, cw), BF16),
            pltpu.VMEM((HEADS, 3, n // 2, rows_out, cw), BF16),
            pltpu.VMEM((HEADS, n // 2, rows_out, cw), BF16),
            pltpu.VMEM((HEADS, n // 2, rows_out, cw), BF16),
            pltpu.VMEM((2, n // 2, rows_out, BS), BF16),
            pltpu.VMEM((3, n // 2, rows_out, BS), BF16),
            pltpu.VMEM((n // 2, rows_out, BS), BF16),
            pltpu.VMEM((n // 2, rows_out, BS), BF16),
            pltpu.VMEM((HEADS, rows_out, cw), F32),
            pltpu.VMEM((rows_out, BS), F32),
            pltpu.SemaphoreType.DMA((HEADS + 1, 3)),
            pltpu.SemaphoreType.DMA((HEADS + 1, 3)),
            pltpu.SemaphoreType.DMA((HEADS + 1, n // 2)),
            pltpu.SemaphoreType.DMA((HEADS + 1, n // 2)),
            pltpu.SemaphoreType.DMA((HEADS + 1,)),
            pltpu.SemaphoreType.DMA((HEADS + 1,)),
        ]
        out_shape += [
            jax.ShapeDtypeStruct((rows_out, 3 * d), F32),
            jax.ShapeDtypeStruct((rows_out, BS), F32),
        ]
    else:
        out_shape += [
            jax.ShapeDtypeStruct((d, 3 * d), F32),
            jax.ShapeDtypeStruct((1, d), F32),
        ]
    dx, w_term, gain_term = pl.pallas_call(
        functools.partial(kernel, n, grad_scale, fused_sum),
        out_shape=out_shape,
        in_specs=[anywhere, anywhere, vmem, anywhere, anywhere],
        out_specs=[anywhere, vmem, vmem],
        scratch_shapes=scratch,
        compiler_params=pltpu.CompilerParams(
            collective_id=0, has_side_effects=True, vmem_limit_bytes=56 * 1024 * 1024
        ),
        cost_estimate=pl.CostEstimate(
            flops=8_000_000_000, bytes_accessed=6_000_000, transcendentals=2_000_000
        ),
    )(
        neighbours,
        inputs.reshape(BLK, BS, d),
        norm_gain.reshape(1, d),
        qkv_weight,
        out_grad.reshape(BLK, BS, d),
    )
    input_grad = dx.reshape(inputs.shape)
    if fused_sum:
        return input_grad, w_term, gain_term[:, 0]
    weight_all = lax.psum(w_term.astype(BF16), "noise").astype(F32)
    gain_all = lax.psum(gain_term[0].astype(BF16), "noise").astype(F32)
    return (
        input_grad,
        lax.psum_scatter(weight_all, "mesh", scatter_dimension=0, tiled=True),
        lax.psum_scatter(gain_all, "mesh", scatter_dimension=0, tiled=True),
    )


def solution(mesh):
    return jax.shard_map(
        functools.partial(per_device, mesh.shape["mesh"], mesh.shape["noise"]),
        mesh=mesh,
        in_specs=(
            P(("groups", "noise"), "mesh", None),
            P(),
            P(),
            P(),
            P(("groups", "noise"), "mesh", None),
        ),
        out_specs=(
            P(("groups", "noise"), "mesh", None),
            P(("groups", "mesh"), None),
            P(("groups", "mesh")),
        ),
        check_vma=False,
    )
```
